256 devices in a mesh: grp: 16 (over x, y), bal: 16 (over z, core).
Axes of the slice: x: 4, y: 4, z: 8, core: 2. Of those that a mesh axis runs over, the one named last changes fastest.
Arguments:
- node_grad: bfloat16 [2048, 49, 128], P(('grp', 'bal')), may hold values from -6 to 6
- coeffs_one: bfloat16 [65536, 29, 128], P(('grp', 'bal')), may hold values from -6 to 6
- coeffs_zero: bfloat16 [65536, 29, 128], P(('grp', 'bal')), may hold values from -6 to 6
- rotations: float32 [65536, 235], P(('grp', 'bal')), may hold values from -2 to 2
- weight_one: bfloat16 [29, 128, 128], replicated, may hold values from -0.5 to 0.5
- weight_two: bfloat16 [29, 128, 128], replicated, may hold values from -0.5 to 0.5
- sources: int32 [65536], P(('grp', 'bal')), may hold values from 0 to 127
- targets: int32 [65536], P(('grp', 'bal')), may hold values from 0 to 127, as said below
- edge_count: int32 [256], P(('grp', 'bal')), may hold values from 4 to 256, as said below
Outputs:
- node_out: float32 [2048, 49, 128], P(('grp', 'bal'))
- grad_one: float32 [29, 128, 128], replicated
- grad_two: float32 [29, 128, 128], replicated
The draws below stay inside these ranges and needn't reach their ends.
Inputs may be any that keep to these rules, and one draw needn't show every extreme that they name: `edge_count`: some device has exactly 256 live slots in every draw. `targets`: the slots of the device at position p of bal target nodes p * 8 to (p + 1) * 8 - 1 of their graph.
All inputs are finite; a program needn't handle non-finite values.
Results may differ from the reference program's by a relative error of at most 0.0047.
Values may be sent and summed in bfloat16 or wider, within the bound.
A program may use at most 128 MiB of HBM per device.

```python
import jax
import jax.numpy as jnp
from jax import lax

C = 128
COEF = 29
SPHERE = 49
WIGNER = 235
NODE_DEV = 8
E_DEV = 256
NODES = 2048
EDGES = 65536
N_GRP = 16
N_BAL = 16


def draw_targets(key, part):
    key = jax.random.fold_in(key, 11)
    total = E_DEV * N_GRP * N_BAL
    position = jnp.arange(total, dtype=jnp.int32) // E_DEV % N_BAL
    offset = jax.random.randint(key, (total,), 0, NODE_DEV, dtype=jnp.int32)
    return position * NODE_DEV + offset


def draw_edge_count(key, part):
    key = jax.random.fold_in(key, 23)
    first_key, second_key = jax.random.split(key)
    devices_all = N_GRP * N_BAL
    factor = jax.random.randint(first_key, (devices_all,), 1, 9, dtype=jnp.int32)
    counts = E_DEV * factor * factor // 64
    fullest = jax.random.randint(second_key, (), 0, devices_all, dtype=jnp.int32)
    return jnp.where(jnp.arange(devices_all, dtype=jnp.int32) == fullest, E_DEV, counts).astype(jnp.int32)


def draw_rotations(key, part):
    key = jax.random.fold_in(key, 37)
    total = E_DEV * N_GRP * N_BAL
    column = jnp.arange(WIGNER, dtype=jnp.int32)
    bounds = jnp.array([1, 10, 35, 70, 115, 170], dtype=jnp.int32)
    degree = jnp.sum((column[:, None] >= bounds[None, :]).astype(jnp.float32), axis=1)
    factor = 0.5 / jnp.sqrt(2.0 * degree + 1.0)
    values = jnp.clip(jax.random.normal(key, (total, WIGNER), jnp.float32), -4.0, 4.0)
    return (values * factor[None, :]).astype(jnp.float32)


def place_ends(values, stream_key, smallest, top_value):
    dims = values.shape
    spot = [jax.random.randint(jax.random.fold_in(stream_key, axis), (), 0, dims[axis]) for axis in range(len(dims))]
    values = values.at[tuple(spot)].set(smallest)
    longest = dims.index(max(dims))
    spot[longest] = (spot[longest] + 1) % dims[longest]
    return values.at[tuple(spot)].set(top_value)


def block_levels(own_key, dims, cuts, low, largest):
    def one(dim, blocks):
        draws = jax.random.uniform(jax.random.fold_in(jax.random.fold_in(own_key, 6), dim), (blocks,), jnp.float32, low / len(cuts), largest / len(cuts))
        return jnp.repeat(jnp.exp(draws), dims[dim] // blocks).reshape((-1,) + (1,) * (len(dims) - dim - 1))

    level = one(*cuts[0])
    for cut in cuts[1:]:
        level = level * one(*cut)
    return level


def bell_draw(own_key, dims, spread, most, pieces=(), held_as=jnp.bfloat16):
    loudness = block_levels(own_key, dims, pieces, -0.22, 0.18) if pieces else 1.0
    values = jax.random.normal(own_key, dims, jnp.float32) * spread * loudness
    return jnp.minimum(jnp.maximum(values, -most), most).astype(held_as)


def setup_inputs(seed: int = 0) -> dict:
    key_list = jax.random.split(jax.random.key(seed), 10)
    node_grad = bell_draw(key_list[0], (NODES, SPHERE, C), 1.0, 6.0, ((0, 256),))
    coeffs_one = bell_draw(key_list[1], (EDGES, COEF, C), 1.0, 6.0, ((0, 256),))
    coeffs_zero = bell_draw(key_list[2], (EDGES, COEF, C), 1.0, 6.0, ((0, 256),))
    rotations = draw_rotations(jax.random.fold_in(key_list[9], 71), 0)
    weight_one = bell_draw(key_list[4], (COEF, C, C), C ** -0.5, 0.5)
    weight_two = bell_draw(key_list[5], (COEF, C, C), C ** -0.5, 0.5)
    sources = place_ends(jax.random.randint(key_list[6], (EDGES,), 0, NODE_DEV * N_BAL), jax.random.fold_in(key_list[6], 1), 0, (NODE_DEV * N_BAL) - 1).astype(jnp.int32)
    targets = draw_targets(jax.random.fold_in(key_list[9], 71), 0)
    edge_count = draw_edge_count(jax.random.fold_in(key_list[9], 71), 0)
    return {"node_grad": node_grad, "coeffs_one": coeffs_one, "coeffs_zero": coeffs_zero, "rotations": rotations, "weight_one": weight_one, "weight_two": weight_two, "sources": sources, "targets": targets, "edge_count": edge_count}


PAIRS = ((7, 13, 19), (19, 24, 29))
ORDER_BASE = (22, 12, 0, 6, 17)


def degree_starts():
    starts = []
    running = 0
    for degree in range(7):
        starts.append(running)
        running = running + (2 * min(degree, 2) + 1) * (2 * degree + 1)
    return starts


def rotation_block(rotation, degree, starts):
    kept = min(degree, 2)
    height = 2 * kept + 1
    width = 2 * degree + 1
    flat = rotation[:, starts[degree]:starts[degree] + height * width]
    return flat.reshape(flat.shape[0], height, width)


def rotate_in(rotation, node_rows):
    starts = degree_starts()
    placed = [None] * 29
    for degree in range(7):
        kept = min(degree, 2)
        block = rotation_block(rotation, degree, starts).astype(jnp.float32)
        turned = jnp.einsum("emk,ekc->emc", block,
                            node_rows[:, degree * degree:(degree + 1) * (degree + 1)].astype(jnp.float32),
                            precision=lax.Precision.HIGHEST)
        for order in range(-kept, kept + 1):
            placed[ORDER_BASE[order + 2] + degree] = turned[:, order + kept]
    return jnp.stack(placed, 1)


def rotate_out(rotation, edge_rows):
    starts = degree_starts()
    parts = []
    for degree in range(7):
        kept = min(degree, 2)
        block = rotation_block(rotation, degree, starts).astype(jnp.float32)
        picked = jnp.stack([edge_rows[:, ORDER_BASE[order + 2] + degree] for order in range(-kept, kept + 1)], 1)
        parts.append(jnp.einsum("emk,emc->ekc", block, picked.astype(jnp.float32),
                                precision=lax.Precision.HIGHEST))
    return jnp.concatenate(parts, 1)


def contract(first_operand, second_operand):
    return jnp.einsum("erc,erd->rcd", first_operand.astype(jnp.float32), second_operand.astype(jnp.float32))


def apply_weight(upstream_rows, weights):
    return jnp.einsum("erd,rcd->erc", upstream_rows.astype(jnp.float32), weights.astype(jnp.float32))


def so2_grads(coeffs, upstream, weights):
    weight_parts = [contract(coeffs[:, :7], upstream[:, :7])]
    back_parts = [apply_weight(upstream[:, :7], weights[:7])]
    for plus_begin, minus_begin, minus_end in PAIRS:
        plus_in = coeffs[:, plus_begin:minus_begin]
        minus_in = coeffs[:, minus_begin:minus_end]
        plus_up = upstream[:, plus_begin:minus_begin]
        minus_up = upstream[:, minus_begin:minus_end]
        cosine_part = weights[plus_begin:minus_begin]
        sine_part = weights[minus_begin:minus_end]
        weight_parts.append(contract(plus_in, plus_up) + contract(minus_in, minus_up))
        weight_parts.append(contract(plus_in, minus_up) - contract(minus_in, plus_up))
        back_parts.append(apply_weight(plus_up, cosine_part) + apply_weight(minus_up, sine_part))
        back_parts.append(apply_weight(minus_up, cosine_part) - apply_weight(plus_up, sine_part))
    return jnp.concatenate(weight_parts, 0), jnp.concatenate(back_parts, 1)


def backward_layer(saved, upstream, weights, rotations, sources, targets, valid_slots):
    group_nodes = NODE_DEV * N_BAL
    group_edges = E_DEV * N_BAL
    saved_groups = saved.reshape(N_GRP, group_edges, COEF, C)
    rotation_groups = rotations.reshape(N_GRP, group_edges, WIGNER)
    upstream_groups = upstream.reshape(N_GRP, group_nodes, SPHERE, C)
    source_groups = sources.reshape(N_GRP, group_edges)
    target_groups = targets.reshape(N_GRP, group_edges)

    def one_group(weight_total, group_items):
        saved_group, rotation_group, up_group, src_group, tgt_group, valid_group = group_items
        turned = rotate_in(rotation_group, up_group[tgt_group].astype(jnp.float32))
        edge_up = jnp.where(valid_group[:, None, None], turned, jnp.zeros((), turned.dtype)).astype(jnp.bfloat16)
        weight_part, edge_back = so2_grads(saved_group, edge_up, weights)
        node_back = rotate_out(rotation_group, edge_back)
        partial_value = jax.ops.segment_sum(node_back, src_group, num_segments=group_nodes)
        return weight_total + weight_part, partial_value

    weight_total, partials = lax.scan(one_group, jnp.zeros((COEF, C, C), jnp.float32),
                                      (saved_groups, rotation_groups, upstream_groups, source_groups,
                                       target_groups, valid_slots))
    return weight_total, partials.reshape(NODES, SPHERE, C)


def reference(node_grad, coeffs_one, coeffs_zero, rotations, weight_one, weight_two, sources, targets, edge_count):
    slot_index = jnp.arange(E_DEV * N_BAL, dtype=jnp.int32)
    slot_owner = slot_index // E_DEV
    counts = edge_count.reshape(N_GRP, N_BAL)
    valid_slots = (slot_index % E_DEV)[None, :] < counts[:, slot_owner]
    grad_two, partial_two = backward_layer(coeffs_one, node_grad, weight_two, rotations, sources, targets, valid_slots)
    upstream_one = node_grad.astype(jnp.float32) + partial_two
    grad_one, partial_one = backward_layer(coeffs_zero, upstream_one.astype(jnp.bfloat16), weight_one, rotations,
                                           sources, targets, valid_slots)
    grad_scale = float(EDGES) ** -0.5
    return upstream_one + partial_one, grad_one * grad_scale, grad_two * grad_scale
```

```python
import functools

import jax
import jax.numpy as jnp
from jax import lax
from jax.experimental import pallas as pl
from jax.experimental.pallas import tpu as pltpu
from jax.sharding import PartitionSpec as P

F32, BF16 = jnp.float32, jnp.bfloat16
MESH = pl.DeviceIdType.MESH

C = 128
COEF = 29
SPHERE = 49
WIGNER = 235
E = 256
T = 8
N_GRP = 16
N_Z = 8
ROWS = 400
SLOTS = 32
BASE = (22, 12, 0, 6, 17)
PAIRS = tuple((7 + i, 13 + i) for i in range(6)) + tuple((19 + i, 24 + i) for i in range(5))


def kept_of(degree):
    return min(degree, 2)


def height_of(degree):
    return 2 * kept_of(degree) + 1


def width_of(degree):
    return 2 * degree + 1


def depth_of(degree):
    return 128 if 16 * width_of(degree) <= 128 else 256


STARTS = []
AT_AT = []
_run = 0
_at = 0
for _l in range(7):
    STARTS.append(_run)
    AT_AT.append(_at)
    _run += height_of(_l) * width_of(_l)
    _at += height_of(_l) * depth_of(_l)
AT_ROWS = _at

PLACE = {r: r for r in range(7)}
for _i, (_p, _q) in enumerate(PAIRS):
    PLACE[_p] = 7 + 2 * _i
    PLACE[_q] = 8 + 2 * _i


def dot_nn(a, b):
    return lax.dot_general(a, b, (((1,), (0,)), ((), ())), preferred_element_type=F32)


def dot_nt(a, b):
    return lax.dot_general(a, b, (((1,), (1,)), ((), ())), preferred_element_type=F32)


def layer_kernel(
    rot_ref, src_ref, tgt_ref, count_ref, u_ref, x_ref, w_ref,
    p_ref, dw_ref,
    rpad, rt, at, gt, xf, sbuf, *dxs,
):
    rpad[:, 128:256] = jnp.zeros((E, 128), F32)
    rpad[:, 0:WIGNER] = rot_ref[...]
    rt[...] = rpad[...].T

    def unpack(e, carry):
        xf[pl.ds(pl.multiple_of(e * 32, 32), COEF), :] = x_ref[e].astype(F32)
        return carry

    lax.fori_loop(0, E, unpack, 0, unroll=8)

    lane = lax.broadcasted_iota(jnp.int32, (T, E), 1)
    spot = lax.broadcasted_iota(jnp.int32, (T, E), 0)
    hit = (spot == tgt_ref[...]) & (lane < count_ref[...])
    hot = jnp.where(hit, 1.0, 0.0).astype(F32)

    for l in range(7):
        width, height, depth = width_of(l), height_of(l), depth_of(l)
        rest = depth - 2 * T * width
        rows = u_ref[T * l * l : T * (l + 1) * (l + 1), :].astype(F32)
        twice = [rows, rows] + ([jnp.zeros((rest, C), F32)] if rest else [])
        ut = jnp.concatenate(twice, 0).T.astype(BF16)
        for m in range(height):
            first = STARTS[l] + m * width
            high, low = [], []
            for k in range(width):
                entry = hot * rt[first + k : first + k + 1, :]
                top = entry.astype(BF16).astype(F32)
                high.append(top)
                low.append(entry - top)
            pieces = high + low + ([jnp.zeros((rest, E), F32)] if rest else [])
            place = PLACE[BASE[m - kept_of(l) + 2] + l]
            turned = dot_nn(ut, jnp.concatenate(pieces, 0).astype(BF16))
            gt[place * C : (place + 1) * C, :] = turned.astype(BF16)

    def coeff(r):
        return xf[pl.ds(r, E, stride=32), :].astype(BF16)

    def put_dx(r, value):
        for l in range(7):
            for m in range(height_of(l)):
                if BASE[m - kept_of(l) + 2] + l == r:
                    dxs[l][:, m * E : (m + 1) * E] = value.astype(BF16)

    for r in range(7):
        g = gt[r * C : (r + 1) * C, :]
        dw_ref[r] = dot_nn(g, coeff(r)).T
        put_dx(r, dot_nn(w_ref[r], g))
    for i, (p, q) in enumerate(PAIRS):
        g = gt[(7 + 2 * i) * C : (9 + 2 * i) * C, :]
        both = dot_nn(g, jnp.concatenate([coeff(p), coeff(q)], 1))
        dw_ref[p] = (both[:C, :C] + both[C:, C:]).T
        dw_ref[q] = (both[C:, :C] - both[:C, C:]).T
        a, b = w_ref[p], w_ref[q]
        block = jnp.concatenate(
            [jnp.concatenate([a, b], 1), jnp.concatenate([-b, a], 1)], 0
        )
        back = dot_nn(block, g)
        put_dx(p, back[:C])
        put_dx(q, back[C:])
    for r in range(COEF, SLOTS):
        dw_ref[r] = jnp.zeros((C, C), F32)

    nodes = lax.broadcasted_iota(jnp.int32, (C, E), 0)
    at_source = jnp.where(nodes == src_ref[...], 1.0, 0.0).astype(F32)
    for l in range(7):
        width, height = width_of(l), height_of(l)
        for k in range(width):
            for m in range(height):
                j = STARTS[l] + m * width + k
                sbuf[l % 2, k * C : (k + 1) * C, m * E : (m + 1) * E] = (
                    at_source * rt[j : j + 1, :]
                ).astype(BF16)
        for k0 in range(0, width, 4):
            k1 = min(k0 + 4, width)
            got = dot_nt(sbuf[l % 2, k0 * C : k1 * C, : height * E], dxs[l][...])
            for k in range(k0, k1):
                row = l * l + k
                p_ref[:, row * T : (row + 1) * T, :] = got[
                    (k - k0) * C : (k - k0 + 1) * C
                ].reshape(C // T, T, C)
    p_ref[:, SPHERE * T : ROWS, :] = jnp.zeros((C // T, ROWS - SPHERE * T, C), F32)


def layer(rot, src, tgt, count, u, x, w):
    scratch = [
        pltpu.VMEM((E, 256), F32),
        pltpu.VMEM((256, E), F32),
        pltpu.VMEM((16, E), BF16),
        pltpu.VMEM((COEF * C, E), BF16),
        pltpu.VMEM((E * 32, C), F32),
        pltpu.VMEM((2, 13 * C, 5 * E), BF16),
    ] + [pltpu.VMEM((C, height_of(l) * E), BF16) for l in range(7)]
    return pl.pallas_call(
        layer_kernel,
        out_shape=(
            jax.ShapeDtypeStruct((C // T, ROWS, C), F32),
            jax.ShapeDtypeStruct((SLOTS, C, C), F32),
        ),
        in_specs=[pl.BlockSpec(memory_space=pltpu.VMEM)] * 7,
        out_specs=(pl.BlockSpec(memory_space=pltpu.VMEM),) * 2,
        scratch_shapes=scratch,
        compiler_params=pltpu.CompilerParams(vmem_limit_bytes=48 * 2**20),
        name="layer",
    )(rot, src, tgt, count, u, x, w)


def greet(q, z, c):
    barrier = pltpu.get_barrier_semaphore()
    b = 2 * z + c

    def signal(grp, bal):
        pl.semaphore_signal(
            barrier, inc=1, device_id={"grp": grp, "bal": bal}, device_id_type=MESH
        )

    signal(q, 2 * z + 1 - c)
    for i in range(1, N_Z):
        signal(q, lax.rem(z + i, N_Z) * 2 + c)
    for i in range(1, N_GRP):
        signal(lax.rem(q + i, N_GRP), b)
    pl.semaphore_wait(barrier, 1 + (N_Z - 1) + (N_GRP - 1))


def remote(src, dst, send, recv, grp, bal):
    return pltpu.make_async_remote_copy(
        src_ref=src, dst_ref=dst, send_sem=send, recv_sem=recv,
        device_id={"grp": grp, "bal": bal}, device_id_type=MESH,
    )


def comm_kernel(last, scale, *refs):
    if last:
        (p_ref, dw_ref, early_ref, part_ref, out_ref, *refs) = refs
    else:
        (p_ref, dw_ref, part_ref, shard_ref, *refs) = refs
    (cbuf, crecv, hop_s, hop_r, dcore, xy_s, xy_r, c_sem, hop_sem, d_sem, xy_sem, *refs) = refs
    if last:
        (zbuf, z_r, slot, z_sem, ag_sem, agxy_sem, fwd_sem) = refs
    q = lax.axis_index("grp")
    b = lax.axis_index("bal")
    z, c = lax.div(b, 2), lax.rem(b, 2)
    other = 2 * z + 1 - c
    greet(q, z, c)

    way = jnp.where(c == 0, N_Z - 1, 1)
    back = N_Z - way
    jobs = [("a", 4), ("b", 3), ("a", 3), ("b", 2), ("a", 2), ("b", 1), ("a", 1), ("own", 0)]

    def dest(chain, dist):
        step = way if chain == "a" else back
        return lax.rem(z + dist * step, N_Z) if dist else z

    sends = []
    for n, (chain, dist) in enumerate(jobs):
        d = dest("b" if chain == "a" else "a", dist)
        cbuf[n] = p_ref[2 * d + 1 - c].astype(BF16)
        copy = remote(cbuf.at[n], crecv.at[n], c_sem.at[0, n], c_sem.at[1, n], q, other)
        copy.start()
        sends.append(copy)
    dcopy = remote(dw_ref.at[pl.ds((1 - c) * 16, 16)], dcore, d_sem.at[0], d_sem.at[1], q, other)
    dcopy.start()

    hops = {}
    order = {("a", 4): 0, ("a", 3): 1, ("a", 2): 2, ("a", 1): 3, ("b", 3): 4, ("b", 2): 5, ("b", 1): 6}

    def chain_step(n):
        chain, dist = jobs[n]
        d = dest(chain, dist)
        sends[n].wait_recv()
        value = p_ref[2 * d + c] + crecv[n].astype(F32)
        before = (chain, dist + 1)
        if chain != "own" and before in order:
            hops[before].wait_recv()
            value += hop_r[order[before]].astype(F32)
        if chain == "own":
            for before in (("a", 1), ("b", 1)):
                hops[before].wait_recv()
                value += hop_r[order[before]].astype(F32)
            part_ref[...] = value
            return
        h = order[(chain, dist)]
        hop_s[h] = value.astype(BF16)
        target = lax.rem(z + (way if chain == "a" else back), N_Z)
        copy = remote(hop_s.at[h], hop_r.at[h], hop_sem.at[0, h], hop_sem.at[1, h], q, 2 * target + c)
        copy.start()
        hops[(chain, dist)] = copy

    chain_step(0)
    chain_step(1)

    dcopy.wait_recv()
    xys = []
    for i in range(1, N_GRP):
        to = lax.rem(q + i, N_GRP)
        xy_s[i - 1] = (dw_ref[c * 16 + to] + dcore[to]).astype(BF16)
        copy = remote(xy_s.at[i - 1], xy_r.at[i - 1], xy_sem.at[0, i - 1], xy_sem.at[1, i - 1], to, b)
        copy.start()
        xys.append(copy)

    chain_step(2)
    chain_step(3)

    def plane_sum():
        total = dw_ref[c * 16 + q] + dcore[q]
        for i in range(1, N_GRP):
            xys[i - 1].wait_recv()
            total += xy_r[i - 1].astype(F32)
        return total

    if not last:
        for n in range(4, 8):
            chain_step(n)
        shard_ref[...] = plane_sum()
        pending = []
    else:
        zbuf[0] = plane_sum()
        zbuf[1] = early_ref[...]
        zs = []
        for i in range(1, N_Z):
            to = lax.rem(z + i, N_Z)
            rows = pl.ds(pl.multiple_of(to * 16, 16), 16)
            copy = remote(zbuf.at[:, rows, :], z_r.at[i - 1], z_sem.at[0, i - 1], z_sem.at[1, i - 1], q, 2 * to + c)
            copy.start()
            zs.append(copy)
        chain_step(4)
        chain_step(5)
        mine = pl.ds(pl.multiple_of(z * 16, 16), 16)
        total = zbuf[:, mine, :]
        for i in range(1, N_Z):
            zs[i - 1].wait_recv()
            total += z_r[i - 1]
        slot[:, mine, :] = (total * scale).astype(BF16)
        ags = []
        for i in range(1, N_Z):
            to = lax.rem(z + i, N_Z)
            copy = remote(slot.at[:, mine, :], slot.at[:, mine, :], ag_sem.at[0, i - 1], ag_sem.at[1, i - 1], q, 2 * to + c)
            copy.start()
            ags.append(copy)
        chain_step(6)
        for i in range(1, N_Z):
            rows = pl.ds(pl.multiple_of(lax.rem(z + N_Z - i, N_Z) * 16, 16), 16)
            remote(slot.at[:, rows, :], slot.at[:, rows, :], ag_sem.at[0, i - 1], ag_sem.at[1, i - 1], q, b).wait_recv()
        for i in range(1, N_Z):
            ags[i - 1].wait_send()
        agxys = []
        for i in range(1, N_GRP):
            to = lax.rem(q + i, N_GRP)
            copy = remote(slot, out_ref.at[:, c * 16 + q], agxy_sem.at[0, i - 1], agxy_sem.at[1, i - 1], to, b)
            copy.start()
            agxys.append(copy)
        out_ref[:, c * 16 + q] = slot[...]
        fwds = [remote(slot, out_ref.at[:, c * 16 + q], fwd_sem.at[0, 0], fwd_sem.at[1, 0], q, other)]
        fwds[0].start()
        chain_step(7)
        for i in range(1, N_GRP):
            came = c * 16 + lax.rem(q + N_GRP - i, N_GRP)
            remote(slot, out_ref.at[:, came], agxy_sem.at[0, i - 1], agxy_sem.at[1, i - 1], q, b).wait_recv()
            copy = remote(out_ref.at[:, came], out_ref.at[:, came], fwd_sem.at[0, i], fwd_sem.at[1, i], q, other)
            copy.start()
            fwds.append(copy)
        for i in range(N_GRP):
            came = (1 - c) * 16 + lax.rem(q + N_GRP - i, N_GRP)
            remote(slot, out_ref.at[:, came], fwd_sem.at[0, i], fwd_sem.at[1, i], q, b).wait_recv()
        pending = zs + agxys + fwds
    for copy in sends + [dcopy] + list(hops.values()) + xys + pending:
        copy.wait_send()


def comm(last, scale, *args):
    dma = pltpu.SemaphoreType.DMA
    scratch = [
        pltpu.VMEM((N_Z, ROWS, C), BF16),
        pltpu.VMEM((N_Z, ROWS, C), BF16),
        pltpu.VMEM((N_Z - 1, ROWS, C), BF16),
        pltpu.VMEM((N_Z - 1, ROWS, C), BF16),
        pltpu.VMEM((16, C, C), F32),
        pltpu.VMEM((N_GRP - 1, C, C), BF16),
        pltpu.VMEM((N_GRP - 1, C, C), BF16),
        dma((2, N_Z)),
        dma((2, N_Z - 1)),
        dma((2,)),
        dma((2, N_GRP - 1)),
    ]
    outs = [jax.ShapeDtypeStruct((ROWS, C), F32)]
    if last:
        scratch += [
            pltpu.VMEM((2, C, C), F32),
            pltpu.VMEM((N_Z - 1, 2, 16, C), F32),
            pltpu.VMEM((2, C, C), BF16),
            dma((2, N_Z - 1)),
            dma((2, N_Z - 1)),
            dma((2, N_GRP - 1)),
            dma((2, N_GRP)),
        ]
        outs.append(jax.ShapeDtypeStruct((2, SLOTS, C, C), BF16))
    else:
        outs.append(jax.ShapeDtypeStruct((C, C), F32))
    return pl.pallas_call(
        functools.partial(comm_kernel, last, scale),
        out_shape=tuple(outs),
        in_specs=[pl.BlockSpec(memory_space=pltpu.VMEM)] * len(args),
        out_specs=(pl.BlockSpec(memory_space=pltpu.VMEM),) * 2,
        scratch_shapes=scratch,
        compiler_params=pltpu.CompilerParams(
            collective_id=1 if last else 0, has_side_effects=True, vmem_limit_bytes=48 * 2**20
        ),
        name="comm_last" if last else "comm_first",
    )(*args)


def on_device(
    node_grad, coeffs_one, coeffs_zero, rotations, weight_one, weight_two, sources, targets, edge_count
):
    scale = float(sources.shape[0] * lax.axis_size("grp") * lax.axis_size("bal")) ** (-0.5)
    src = sources.reshape(1, E)
    tgt = (targets - lax.axis_index("bal") * T).reshape(1, E)
    count = edge_count.reshape(1, 1)
    top = jnp.transpose(node_grad, (1, 0, 2)).reshape(SPHERE * T, C).astype(F32)
    top = jnp.pad(top, ((0, ROWS - SPHERE * T), (0, 0)))

    sums_two, dw_two = layer(rotations, src, tgt, count, top, coeffs_one, weight_two)
    part_two, shard_two = comm(False, scale, sums_two, dw_two)
    up_one = top + part_two
    sums_one, dw_one = layer(
        rotations, src, tgt, count, up_one.astype(BF16), coeffs_zero, weight_one
    )
    part_one, grads = comm(True, scale, sums_one, dw_one, shard_two)
    node_out = (up_one + part_one)[: SPHERE * T].reshape(SPHERE, T, C).transpose(1, 0, 2)
    return node_out, grads[0, :COEF].astype(F32), grads[1, :COEF].astype(F32)


def solution(mesh):
    both = P(("grp", "bal"))
    return jax.shard_map(
        on_device,
        mesh=mesh,
        in_specs=(
            P(("grp", "bal"), None, None),
            P(("grp", "bal"), None, None),
            P(("grp", "bal"), None, None),
            P(("grp", "bal"), None),
            P(),
            P(),
            both,
            both,
            both,
        ),
        out_specs=(P(("grp", "bal"), None, None), P(), P()),
        check_vma=False,
    )
```

```python
import functools

import jax
import jax.numpy as jnp
from jax import lax
from jax.experimental import pallas as pl
from jax.experimental.pallas import tpu as pltpu
from jax.sharding import PartitionSpec as P

F32, BF16 = jnp.float32, jnp.bfloat16
MESH = pl.DeviceIdType.MESH

C = 128
COEF = 29
SPHERE = 49
WIGNER = 235
E = 256
T = 8
N_GRP = 16
N_Z = 8
ROWS = 400
SLOTS = 32
BASE = (22, 12, 0, 6, 17)
PAIRS = tuple((7 + i, 13 + i) for i in range(6)) + tuple((19 + i, 24 + i) for i in range(5))


def kept_of(degree):
    return min(degree, 2)


def height_of(degree):
    return 2 * kept_of(degree) + 1


def width_of(degree):
    return 2 * degree + 1


def depth_of(degree):
    return 128 if 16 * width_of(degree) <= 128 else 256


STARTS = []
AT_AT = []
_run = 0
_at = 0
for _l in range(7):
    STARTS.append(_run)
    AT_AT.append(_at)
    _run += height_of(_l) * width_of(_l)
    _at += height_of(_l) * depth_of(_l)
AT_ROWS = _at

PLACE = {r: r for r in range(7)}
for _i, (_p, _q) in enumerate(PAIRS):
    PLACE[_p] = 7 + 2 * _i
    PLACE[_q] = 8 + 2 * _i


def dot_nn(a, b):
    return lax.dot_general(a, b, (((1,), (0,)), ((), ())), preferred_element_type=F32)


def dot_nt(a, b):
    return lax.dot_general(a, b, (((1,), (1,)), ((), ())), preferred_element_type=F32)


SINGLES = tuple(range(7))
ITEMS = SINGLES + PAIRS
CHUNKS = (((6,), 288, 112), ((4, 5), 128, 160), ((0, 1, 2, 3), 0, 128))
LIVE = SPHERE * T
OFFSETS = (
    (1, 0), (0, 1), (3, 0), (0, 3), (1, 1), (3, 3), (1, 3), (3, 1),
    (2, 0), (0, 2), (2, 1), (1, 2), (2, 3), (3, 2), (2, 2),
)
HOP = {("a", 4): 0, ("a", 3): 1, ("a", 2): 2, ("a", 1): 3, ("b", 3): 4, ("b", 2): 5, ("b", 1): 6}
STEPS = (
    (("a", 4), ("b", 3)), (("a", 3), ("b", 2)), (("a", 2), ("b", 1)), (("a", 1),), (("own", 0),),
)


def remote(src, dst, send, recv, grp, bal):
    return pltpu.make_async_remote_copy(
        src_ref=src, dst_ref=dst, send_sem=send, recv_sem=recv,
        device_id={"grp": grp, "bal": bal}, device_id_type=MESH,
    )


def kernel(
    scale,
    rot_ref, src_ref, tgt_ref, count_ref, top_ref, x_two, x_one, w_two, w_one,
    node_ref, out_ref,
    xs, ws, up, at, gt, sbuf, p, cbuf, crecv, hop_s, hop_r,
    dw, dcore, xy_s, xy_r, zbuf, z_r, slot,
    in_sem, c_sem, hop_sem, d_sem, xy_sem, z_sem, ag_sem, agxy_sem, fwd_sem,
    *dxs,
):
    q = lax.axis_index("grp")
    b = lax.axis_index("bal")
    z, c = lax.div(b, 2), lax.rem(b, 2)
    px, py = lax.div(q, 4), lax.rem(q, 4)
    other = 2 * z + 1 - c

    def plane(dx, dy):
        return lax.rem(px + dx, 4) * 4 + lax.rem(py + dy, 4)

    ahead = [plane(dx, dy) for dx, dy in OFFSETS]
    behind = [plane(4 - dx, 4 - dy) for dx, dy in OFFSETS]

    barrier = pltpu.get_barrier_semaphore()

    def signal(grp, bal):
        pl.semaphore_signal(
            barrier, inc=1, device_id={"grp": grp, "bal": bal}, device_id_type=MESH
        )

    signal(q, other)
    for i in range(1, N_Z):
        signal(q, lax.rem(z + i, N_Z) * 2 + c)
    for to in ahead:
        signal(to, b)

    loads = {}
    for n, (name, src, dst) in enumerate((
        ("w0", w_two, ws.at[0]), ("x0", x_two, xs.at[0]), ("w1", w_one, ws.at[1]), ("x1", x_one, xs.at[1]),
    )):
        loads[name] = pltpu.make_async_copy(src, dst, in_sem.at[n])
        loads[name].start()

    up[0:LIVE] = top_ref[...].astype(F32)
    up[LIVE:ROWS] = jnp.zeros((ROWS - LIVE, C), F32)
    p[:, :, LIVE:ROWS] = jnp.zeros((N_Z, 2, ROWS - LIVE, C), F32)

    def front(layer):
        if layer == 0:
            lane = lax.broadcasted_iota(jnp.int32, (T, E), 1)
            spot = lax.broadcasted_iota(jnp.int32, (T, E), 0)
            hit = (spot == tgt_ref[...] - b * T) & (lane < count_ref[...])
            hot = jnp.where(hit, 1.0, 0.0).astype(F32)
        for l in range(7):
            width, height, depth = width_of(l), height_of(l), depth_of(l)
            rest = depth - 2 * T * width
            rows = up[T * l * l : T * (l + 1) * (l + 1), :]
            twice = [rows, rows] + ([jnp.zeros((rest, C), F32)] if rest else [])
            ut = jnp.concatenate(twice, 0).T.astype(BF16)
            for m in range(height):
                first = AT_AT[l] + m * depth
                if layer == 0:
                    high, low = [], []
                    for k in range(width):
                        j = STARTS[l] + m * width + k
                        entry = hot * rot_ref[j : j + 1, :]
                        top = entry.astype(BF16).astype(F32)
                        high.append(top)
                        low.append(entry - top)
                    pieces = high + low + ([jnp.zeros((rest, E), F32)] if rest else [])
                    at[first : first + depth, :] = jnp.concatenate(pieces, 0).astype(BF16)
                place = PLACE[BASE[m - kept_of(l) + 2] + l]
                turned = dot_nn(ut, at[first : first + depth, :])
                gt[place * C : (place + 1) * C, :] = turned.astype(BF16)

    def weight_grads(layer, items):
        for item in items:
            if isinstance(item, int):
                g = gt[item * C : (item + 1) * C, :]
                dw[layer, item] = dot_nn(g, xs[layer, item]).T
                continue
            r, s = item
            g = gt[PLACE[r] * C : (PLACE[r] + 2) * C, :]
            both = dot_nn(g, jnp.concatenate([xs[layer, r], xs[layer, s]], 1))
            dw[layer, r] = (both[:C, :C] + both[C:, C:]).T
            dw[layer, s] = (both[C:, :C] - both[:C, C:]).T

    for layer in range(2):
        for r in range(COEF, SLOTS):
            dw[layer, r] = jnp.zeros((C, C), F32)

    def put_dx(r, value):
        high = value.astype(BF16)
        low = (value - high.astype(F32)).astype(BF16)
        for l in range(7):
            for m in range(height_of(l)):
                if BASE[m - kept_of(l) + 2] + l == r:
                    dxs[l][0:C, m * E : (m + 1) * E] = high
                    dxs[l][C : 2 * C, m * E : (m + 1) * E] = low

    def edge_back(layer):
        for item in ITEMS:
            if isinstance(item, int):
                put_dx(item, dot_nn(ws[layer, item], gt[item * C : (item + 1) * C, :]))
                continue
            r, s = item
            g = gt[PLACE[r] * C : (PLACE[r] + 2) * C, :]
            cosine, sine = ws[layer, r], ws[layer, s]
            block = jnp.concatenate(
                [jnp.concatenate([cosine, sine], 1), jnp.concatenate([-sine, cosine], 1)], 0
            )
            back = dot_nn(block, g)
            put_dx(r, back[:C])
            put_dx(s, back[C:])

    def outward(layer, chunk):
        degrees, begin, count = CHUNKS[chunk]
        for l in degrees:
            width, height = width_of(l), height_of(l)
            if layer == 0:
                nodes = lax.broadcasted_iota(jnp.int32, (C, E), 0)
                at_source = jnp.where(nodes == src_ref[...], 1.0, 0.0).astype(F32)
                for k in range(width):
                    for m in range(height):
                        j = STARTS[l] + m * width + k
                        sbuf[l][k * C : (k + 1) * C, m * E : (m + 1) * E] = (
                            at_source * rot_ref[j : j + 1, :]
                        ).astype(BF16)
            for k0 in range(0, width, 4):
                k1 = min(k0 + 4, width)
                got = dot_nt(sbuf[l][k0 * C : k1 * C, :], dxs[l][...])
                got = got[:, :C] + got[:, C:]
                for k in range(k0, k1):
                    row = l * l + k
                    p[:, :, row * T : (row + 1) * T, :] = got[
                        (k - k0) * C : (k - k0 + 1) * C
                    ].reshape(N_Z, 2, T, C)

    way = jnp.where(c == 0, N_Z - 1, 1)
    step_of = {"a": way, "b": N_Z - way, "own": way}
    started = []

    def start(copy):
        copy.start()
        started.append(copy)
        return copy

    def rows_of(chunk):
        _, begin, count = CHUNKS[chunk]
        return slice(begin, begin + count)

    cores, hops, cross, planes, lines, spreads, wides = {}, {}, {}, {}, {}, {}, {}

    def core_send(layer, chunk):
        rows = rows_of(chunk)
        cbuf[layer, :, rows] = p[:, 1 - c, rows].astype(BF16)
        view = (layer, slice(None), pl.ds(rows.start, rows.stop - rows.start))
        cores[layer, chunk] = start(remote(
            cbuf.at[view], crecv.at[view], c_sem.at[0, layer, chunk], c_sem.at[1, layer, chunk], q, other
        ))

    def chain(layer, chunk, step):
        rows = rows_of(chunk)
        if step == 0:
            cores[layer, chunk].wait_recv()
        for name, dist in STEPS[step]:
            d = lax.rem(z + dist * step_of[name], N_Z)
            value = p[d, c, rows] + crecv[layer, d, rows].astype(F32)
            before = (("a", 1), ("b", 1)) if name == "own" else ((name, dist + 1),)
            for key in before:
                if key in HOP:
                    hops[layer, chunk, key].wait_recv()
                    value += hop_r[layer, HOP[key], rows].astype(F32)
            if name == "own":
                live = min(rows.stop, LIVE) - rows.start
                kept = slice(rows.start, rows.start + live)
                if layer == 0:
                    up[kept] = up[kept] + value[:live]
                else:
                    node_ref[kept] = up[kept] + value[:live]
                continue
            h = HOP[name, dist]
            hop_s[layer, h, rows] = value.astype(BF16)
            view = (layer, h, pl.ds(rows.start, rows.stop - rows.start))
            to = 2 * lax.rem(z + step_of[name], N_Z) + c
            hops[layer, chunk, (name, dist)] = start(remote(
                hop_s.at[view], hop_r.at[view], hop_sem.at[0, layer, chunk, h], hop_sem.at[1, layer, chunk, h], q, to
            ))

    def d_send(layer):
        half = pl.ds((1 - c) * 16, 16)
        cross[layer] = start(remote(
            dw.at[layer, half], dcore.at[layer], d_sem.at[0, layer], d_sem.at[1, layer], q, other
        ))

    def xy_send(layer):
        cross[layer].wait_recv()
        for i, to in enumerate(ahead):
            xy_s[layer, i] = (dw[layer, c * 16 + to] + dcore[layer, to]).astype(BF16)
            planes[layer, i] = start(remote(
                xy_s.at[layer, i], xy_r.at[layer, i], xy_sem.at[0, layer, i], xy_sem.at[1, layer, i], to, b
            ))

    def z_send(layer):
        total = dw[layer, c * 16 + q] + dcore[layer, q]
        for i in range(N_GRP - 1):
            planes[layer, i].wait_recv()
            total += xy_r[layer, i].astype(F32)
        zbuf[layer] = total
        for i in range(1, N_Z):
            to = lax.rem(z + i, N_Z)
            rows = pl.ds(pl.multiple_of(to * 16, 16), 16)
            lines[layer, i] = start(remote(
                zbuf.at[layer, rows], z_r.at[layer, i - 1], z_sem.at[0, layer, i - 1], z_sem.at[1, layer, i - 1],
                q, 2 * to + c,
            ))

    mine = pl.ds(pl.multiple_of(z * 16, 16), 16)

    def z_sum(layer):
        total = zbuf[layer, mine, :]
        for i in range(1, N_Z):
            lines[layer, i].wait_recv()
            total += z_r[layer, i - 1]
        slot[layer, mine, :] = (total * scale).astype(BF16)
        for i in range(1, N_Z):
            to = lax.rem(z + i, N_Z)
            spreads[layer, i] = start(remote(
                slot.at[layer, mine], slot.at[layer, mine], ag_sem.at[0, layer, i - 1], ag_sem.at[1, layer, i - 1],
                q, 2 * to + c,
            ))

    def gather(layer):
        for i in range(1, N_Z):
            rows = pl.ds(pl.multiple_of(lax.rem(z + N_Z - i, N_Z) * 16, 16), 16)
            view = slot.at[layer, rows]
            remote(view, view, ag_sem.at[0, layer, i - 1], ag_sem.at[1, layer, i - 1], q, other).wait_recv()
        for i, to in enumerate(ahead):
            wides[layer, i] = start(remote(
                slot.at[layer], out_ref.at[layer, c * 16 + q], agxy_sem.at[0, layer, i], agxy_sem.at[1, layer, i], to, b
            ))
        start(remote(
            slot.at[layer], out_ref.at[layer, c * 16 + q], fwd_sem.at[0, layer, 15], fwd_sem.at[1, layer, 15], q, other
        ))
        out_ref[layer, c * 16 + q] = slot[layer]

    def forward(layer):
        for i, came in enumerate(behind):
            view = out_ref.at[layer, c * 16 + came]
            remote(slot.at[layer], view, agxy_sem.at[0, layer, i], agxy_sem.at[1, layer, i], q, other).wait_recv()
            start(remote(view, view, fwd_sem.at[0, layer, i], fwd_sem.at[1, layer, i], q, other))

    def finish(layer):
        for i, came in enumerate(behind + [q]):
            view = out_ref.at[layer, (1 - c) * 16 + came]
            remote(slot.at[layer], view, fwd_sem.at[0, layer, i], fwd_sem.at[1, layer, i], q, other).wait_recv()

    front(0)
    loads["w0"].wait()
    edge_back(0)
    outward(0, 0)
    pl.semaphore_wait(barrier, 1 + (N_Z - 1) + (N_GRP - 1))
    core_send(0, 0)
    outward(0, 1)
    core_send(0, 1)
    chain(0, 0, 0)
    outward(0, 2)
    core_send(0, 2)
    chain(0, 1, 0)
    chain(0, 0, 1)
    loads["x0"].wait()
    weight_grads(0, ITEMS[:9])
    chain(0, 2, 0)
    chain(0, 1, 1)
    chain(0, 0, 2)
    weight_grads(0, ITEMS[9:])
    chain(0, 2, 1)
    chain(0, 1, 2)
    chain(0, 0, 3)
    d_send(0)
    chain(0, 2, 2)
    chain(0, 1, 3)
    chain(0, 0, 4)
    xy_send(0)
    chain(0, 2, 3)
    chain(0, 1, 4)
    chain(0, 2, 4)

    front(1)
    z_send(0)
    loads["x1"].wait()
    weight_grads(1, ITEMS)
    d_send(1)
    z_sum(0)
    loads["w1"].wait()
    edge_back(1)
    xy_send(1)
    outward(1, 0)
    core_send(1, 0)
    outward(1, 1)
    core_send(1, 1)
    gather(0)
    chain(1, 0, 0)
    outward(1, 2)
    core_send(1, 2)
    chain(1, 1, 0)
    chain(1, 0, 1)
    z_send(1)
    chain(1, 2, 0)
    chain(1, 1, 1)
    chain(1, 0, 2)
    z_sum(1)
    chain(1, 2, 1)
    chain(1, 1, 2)
    chain(1, 0, 3)
    gather(1)
    chain(1, 2, 2)
    chain(1, 1, 3)
    chain(1, 0, 4)
    forward(0)
    chain(1, 2, 3)
    chain(1, 1, 4)
    chain(1, 2, 4)
    forward(1)
    finish(0)
    finish(1)
    for copy in started:
        copy.wait_send()


def both_layers(scale, rot, src, tgt, count, top, x_two, x_one, w_two, w_one):
    dma = pltpu.SemaphoreType.DMA
    vmem = pl.BlockSpec(memory_space=pltpu.VMEM)
    hbm = pl.BlockSpec(memory_space=pl.ANY)
    peers = N_GRP - 1
    scratch = [
        pltpu.VMEM((2, COEF, E, C), BF16),
        pltpu.VMEM((2, COEF, C, C), BF16),
        pltpu.VMEM((ROWS, C), F32),
        pltpu.VMEM((AT_ROWS, E), BF16),
        pltpu.VMEM((COEF * C, E), BF16),
        [pltpu.VMEM((width_of(l) * C, height_of(l) * E), BF16) for l in range(7)],
        pltpu.VMEM((N_Z, 2, ROWS, C), F32),
        pltpu.VMEM((2, N_Z, ROWS, C), BF16),
        pltpu.VMEM((2, N_Z, ROWS, C), BF16),
        pltpu.VMEM((2, N_Z - 1, ROWS, C), BF16),
        pltpu.VMEM((2, N_Z - 1, ROWS, C), BF16),
        pltpu.VMEM((2, SLOTS, C, C), F32),
        pltpu.VMEM((2, 16, C, C), F32),
        pltpu.VMEM((2, peers, C, C), BF16),
        pltpu.VMEM((2, peers, C, C), BF16),
        pltpu.VMEM((2, C, C), F32),
        pltpu.VMEM((2, N_Z - 1, 16, C), F32),
        pltpu.VMEM((2, C, C), BF16),
        dma((4,)),
        dma((2, 2, len(CHUNKS))),
        dma((2, 2, len(CHUNKS), N_Z - 1)),
        dma((2, 2)),
        dma((2, 2, peers)),
        dma((2, 2, N_Z - 1)),
        dma((2, 2, N_Z - 1)),
        dma((2, 2, peers)),
        dma((2, 2, N_GRP)),
    ] + [pltpu.VMEM((2 * C, height_of(l) * E), BF16) for l in range(7)]
    return pl.pallas_call(
        functools.partial(kernel, scale),
        out_shape=(
            jax.ShapeDtypeStruct((LIVE, C), F32),
            jax.ShapeDtypeStruct((2, SLOTS, C, C), BF16),
        ),
        in_specs=[vmem] * 5 + [hbm] * 4,
        out_specs=(vmem, vmem),
        scratch_shapes=scratch,
        compiler_params=pltpu.CompilerParams(
            collective_id=0, has_side_effects=True, vmem_limit_bytes=58 * 2**20
        ),
        name="both_layers",
    )(rot, src, tgt, count, top, x_two, x_one, w_two, w_one)


def on_device(
    node_grad, coeffs_one, coeffs_zero, rotations, weight_one, weight_two, sources, targets, edge_count
):
    scale = float(sources.shape[0] * lax.axis_size("grp") * lax.axis_size("bal")) ** (-0.5)
    node, grads = both_layers(
        scale,
        rotations.T,
        sources.reshape(1, E),
        targets.reshape(1, E),
        edge_count.reshape(1, 1),
        jnp.transpose(node_grad, (1, 0, 2)).reshape(LIVE, C),
        jnp.transpose(coeffs_one, (1, 0, 2)),
        jnp.transpose(coeffs_zero, (1, 0, 2)),
        weight_two,
        weight_one,
    )
    node_out = node.reshape(SPHERE, T, C).transpose(1, 0, 2)
    return node_out, grads[1, :COEF].astype(F32), grads[0, :COEF].astype(F32)


def solution(mesh):
    both = P(("grp", "bal"))
    return jax.shard_map(
        on_device,
        mesh=mesh,
        in_specs=(
            P(("grp", "bal"), None, None),
            P(("grp", "bal"), None, None),
            P(("grp", "bal"), None, None),
            P(("grp", "bal"), None),
            P(),
            P(),
            both,
            both,
            both,
        ),
        out_specs=(P(("grp", "bal"), None, None), P(), P()),
        check_vma=False,
    )
```

```python
import functools

import jax
import jax.numpy as jnp
from jax import lax
from jax.experimental import pallas as pl
from jax.experimental.pallas import tpu as pltpu
from jax.sharding import PartitionSpec as P

F32, BF16 = jnp.float32, jnp.bfloat16
MESH = pl.DeviceIdType.MESH

C = 128
COEF = 29
SPHERE = 49
WIGNER = 235
E = 256
T = 8
N_GRP = 16
N_Z = 8
ROWS = 400
SLOTS = 32
BASE = (22, 12, 0, 6, 17)
PAIRS = tuple((7 + i, 13 + i) for i in range(6)) + tuple((19 + i, 24 + i) for i in range(5))


def kept_of(degree):
    return min(degree, 2)


def height_of(degree):
    return 2 * kept_of(degree) + 1


def width_of(degree):
    return 2 * degree + 1


def depth_of(degree):
    return 128 if 16 * width_of(degree) <= 128 else 256


STARTS = []
AT_AT = []
_run = 0
_at = 0
for _l in range(7):
    STARTS.append(_run)
    AT_AT.append(_at)
    _run += height_of(_l) * width_of(_l)
    _at += height_of(_l) * depth_of(_l)
AT_ROWS = _at

PLACE = {r: r for r in range(7)}
for _i, (_p, _q) in enumerate(PAIRS):
    PLACE[_p] = 7 + 2 * _i
    PLACE[_q] = 8 + 2 * _i


def dot_nn(a, b):
    return lax.dot_general(a, b, (((1,), (0,)), ((), ())), preferred_element_type=F32)


def dot_nt(a, b):
    return lax.dot_general(a, b, (((1,), (1,)), ((), ())), preferred_element_type=F32)


SINGLES = tuple(range(7))
PARTS = (SINGLES + PAIRS[6:], PAIRS[:6])
ITEMS = PARTS[0] + PARTS[1]
PART_SLOTS = ((0, 9), (9, 7))
CHUNKS = (((6,), 288, 112), ((4, 5), 128, 160), ((0, 1, 2, 3), 0, 128))
LIVE = SPHERE * T
OFFSETS = (
    (1, 0), (0, 1), (3, 0), (0, 3), (1, 1), (3, 3), (1, 3), (3, 1),
    (2, 0), (0, 2), (2, 1), (1, 2), (2, 3), (3, 2), (2, 2),
)
HOP = {("a", 4): 0, ("a", 3): 1, ("a", 2): 2, ("a", 1): 3, ("b", 3): 4, ("b", 2): 5, ("b", 1): 6}


def slot_of(r):
    if 7 <= r <= 18 or r >= 30:
        j = r - 7 if r <= 18 else r - 18
        return j // 7, 9 + j % 7
    a = r if r < 7 else r - 12
    return a // 9, a % 9


STEPS = (
    (("a", 4), ("b", 3)), (("a", 3), ("b", 2)), (("a", 2), ("b", 1)), (("a", 1),), (("own", 0),),
)


def remote(src, dst, send, recv, grp, bal):
    return pltpu.make_async_remote_copy(
        src_ref=src, dst_ref=dst, send_sem=send, recv_sem=recv,
        device_id={"grp": grp, "bal": bal}, device_id_type=MESH,
    )


def kernel(
    scale,
    rot_ref, src_ref, tgt_ref, count_ref, top_ref, x_two, x_one, w_two, w_one,
    node_ref, out_ref,
    xs, ws, up, at, gt, sbuf, p, cbuf, crecv, hop_s, hop_r,
    dw, dcore, xy_s, xy_r, zbuf, z_r, slot, gath,
    in_sem, c_sem, hop_sem, d_sem, xy_sem, z_sem, ag_sem, agxy_sem, fwd_sem,
    *dxs,
):
    q = lax.axis_index("grp")
    b = lax.axis_index("bal")
    z, c = lax.div(b, 2), lax.rem(b, 2)
    px, py = lax.div(q, 4), lax.rem(q, 4)
    other = 2 * z + 1 - c

    def plane(dx, dy):
        return lax.rem(px + dx, 4) * 4 + lax.rem(py + dy, 4)

    ahead = [plane(dx, dy) for dx, dy in OFFSETS]
    behind = [plane(4 - dx, 4 - dy) for dx, dy in OFFSETS]

    barrier = pltpu.get_barrier_semaphore()

    def signal(grp, bal):
        pl.semaphore_signal(
            barrier, inc=1, device_id={"grp": grp, "bal": bal}, device_id_type=MESH
        )

    signal(q, other)
    for i in range(1, N_Z):
        signal(q, lax.rem(z + i, N_Z) * 2 + c)
    for to in ahead:
        signal(to, b)

    loads = {}
    for n, (name, src, dst) in enumerate((
        ("w0", w_two, ws.at[0]), ("x0", x_two, xs.at[0]), ("w1", w_one, ws.at[1]), ("x1", x_one, xs.at[1]),
    )):
        loads[name] = pltpu.make_async_copy(src, dst, in_sem.at[n])
        loads[name].start()

    up[0:LIVE] = top_ref[...].astype(F32)
    up[LIVE:ROWS] = jnp.zeros((ROWS - LIVE, C), F32)
    p[:, :, LIVE:ROWS] = jnp.zeros((N_Z, 2, ROWS - LIVE, C), F32)

    def front(layer):
        if layer == 0:
            lane = lax.broadcasted_iota(jnp.int32, (T, E), 1)
            spot = lax.broadcasted_iota(jnp.int32, (T, E), 0)
            hit = (spot == tgt_ref[...] - b * T) & (lane < count_ref[...])
            hot = jnp.where(hit, 1.0, 0.0).astype(F32)
        for l in range(7):
            width, height, depth = width_of(l), height_of(l), depth_of(l)
            rest = depth - 2 * T * width
            rows = up[T * l * l : T * (l + 1) * (l + 1), :]
            twice = [rows, rows] + ([jnp.zeros((rest, C), F32)] if rest else [])
            ut = jnp.concatenate(twice, 0).T.astype(BF16)
            for m in range(height):
                first = AT_AT[l] + m * depth
                if layer == 0:
                    high, low = [], []
                    for k in range(width):
                        j = STARTS[l] + m * width + k
                        entry = hot * rot_ref[j : j + 1, :]
                        top = entry.astype(BF16).astype(F32)
                        high.append(top)
                        low.append(entry - top)
                    pieces = high + low + ([jnp.zeros((rest, E), F32)] if rest else [])
                    at[first : first + depth, :] = jnp.concatenate(pieces, 0).astype(BF16)
                place = PLACE[BASE[m - kept_of(l) + 2] + l]
                turned = dot_nn(ut, at[first : first + depth, :])
                gt[place * C : (place + 1) * C, :] = turned.astype(BF16)

    def weight_grads(layer, items):
        for item in items:
            if isinstance(item, int):
                g = gt[item * C : (item + 1) * C, :]
                dw[(layer, *slot_of(item))] = dot_nn(g, xs[layer, item]).T
                continue
            r, s = item
            g = gt[PLACE[r] * C : (PLACE[r] + 2) * C, :]
            both = dot_nn(g, jnp.concatenate([xs[layer, r], xs[layer, s]], 1))
            dw[(layer, *slot_of(r))] = (both[:C, :C] + both[C:, C:]).T
            dw[(layer, *slot_of(s))] = (both[C:, :C] - both[:C, C:]).T

    for layer in range(2):
        for r in range(COEF, SLOTS):
            dw[(layer, *slot_of(r))] = jnp.zeros((C, C), F32)

    def put_dx(r, value):
        high = value.astype(BF16)
        low = (value - high.astype(F32)).astype(BF16)
        for l in range(7):
            for m in range(height_of(l)):
                if BASE[m - kept_of(l) + 2] + l == r:
                    dxs[l][0:C, m * E : (m + 1) * E] = high
                    dxs[l][C : 2 * C, m * E : (m + 1) * E] = low

    def edge_back(layer):
        for item in ITEMS:
            if isinstance(item, int):
                put_dx(item, dot_nn(ws[layer, item], gt[item * C : (item + 1) * C, :]))
                continue
            r, s = item
            g = gt[PLACE[r] * C : (PLACE[r] + 2) * C, :]
            cosine, sine = ws[layer, r], ws[layer, s]
            block = jnp.concatenate(
                [jnp.concatenate([cosine, sine], 1), jnp.concatenate([-sine, cosine], 1)], 0
            )
            back = dot_nn(block, g)
            put_dx(r, back[:C])
            put_dx(s, back[C:])

    def outward(layer, chunk):
        degrees, begin, count = CHUNKS[chunk]
        for l in degrees:
            width, height = width_of(l), height_of(l)
            if layer == 0:
                nodes = lax.broadcasted_iota(jnp.int32, (C, E), 0)
                at_source = jnp.where(nodes == src_ref[...], 1.0, 0.0).astype(F32)
                for k in range(width):
                    for m in range(height):
                        j = STARTS[l] + m * width + k
                        sbuf[l][k * C : (k + 1) * C, m * E : (m + 1) * E] = (
                            at_source * rot_ref[j : j + 1, :]
                        ).astype(BF16)
            for k0 in range(0, width, 4):
                k1 = min(k0 + 4, width)
                got = dot_nt(sbuf[l][k0 * C : k1 * C, :], dxs[l][...])
                got = got[:, :C] + got[:, C:]
                for k in range(k0, k1):
                    row = l * l + k
                    p[:, :, row * T : (row + 1) * T, :] = got[
                        (k - k0) * C : (k - k0 + 1) * C
                    ].reshape(N_Z, 2, T, C)

    way = jnp.where(c == 0, N_Z - 1, 1)
    step_of = {"a": way, "b": N_Z - way, "own": way}
    started = []

    def start(copy):
        copy.start()
        started.append(copy)
        return copy

    def rows_of(chunk):
        _, begin, count = CHUNKS[chunk]
        return slice(begin, begin + count)

    cores, hops, cross, planes, lines, spreads, wides = {}, {}, {}, {}, {}, {}, {}

    def core_send(layer, chunk):
        rows = rows_of(chunk)
        cbuf[layer, :, rows] = p[:, 1 - c, rows].astype(BF16)
        view = (layer, slice(None), pl.ds(rows.start, rows.stop - rows.start))
        cores[layer, chunk] = start(remote(
            cbuf.at[view], crecv.at[view], c_sem.at[0, layer, chunk], c_sem.at[1, layer, chunk], q, other
        ))

    def chain(layer, chunk, step):
        rows = rows_of(chunk)
        if step == 0:
            cores[layer, chunk].wait_recv()
        for name, dist in STEPS[step]:
            d = lax.rem(z + dist * step_of[name], N_Z)
            value = p[d, c, rows] + crecv[layer, d, rows].astype(F32)
            before = (("a", 1), ("b", 1)) if name == "own" else ((name, dist + 1),)
            for key in before:
                if key in HOP:
                    hops[layer, chunk, key].wait_recv()
                    value += hop_r[layer, HOP[key], rows].astype(F32)
            if name == "own":
                live = min(rows.stop, LIVE) - rows.start
                kept = slice(rows.start, rows.start + live)
                if layer == 0:
                    up[kept] = up[kept] + value[:live]
                else:
                    node_ref[kept] = up[kept] + value[:live]
                continue
            h = HOP[name, dist]
            hop_s[layer, h, rows] = value.astype(BF16)
            view = (layer, h, pl.ds(rows.start, rows.stop - rows.start))
            to = 2 * lax.rem(z + step_of[name], N_Z) + c
            hops[layer, chunk, (name, dist)] = start(remote(
                hop_s.at[view], hop_r.at[view], hop_sem.at[0, layer, chunk, h], hop_sem.at[1, layer, chunk, h], q, to
            ))

    def d_send(layer, part):
        first, count = PART_SLOTS[part]
        view = pl.ds(first, count)
        cross[layer, part] = start(remote(
            dw.at[layer, 1 - c, view], dcore.at[layer, view], d_sem.at[0, layer, part], d_sem.at[1, layer, part], q, other
        ))

    def xy_send(layer, part):
        cross[layer, part].wait_recv()
        first, count = PART_SLOTS[part]
        for i in range(count):
            to = first + lax.rem(q + i, count)

            @pl.when(to != q)
            def _():
                there = lax.rem(to - q + N_GRP, N_GRP) - 1
                here = lax.rem(q - to + N_GRP, N_GRP) - 1
                xy_s[layer, there] = (dw[layer, c, to] + dcore[layer, to]).astype(BF16)
                remote(
                    xy_s.at[layer, there], xy_r.at[layer, here], xy_sem.at[0, layer], xy_sem.at[1, layer], to, b
                ).start()

    def plane_all(layer):
        return remote(xy_s.at[layer], xy_r.at[layer], xy_sem.at[0, layer], xy_sem.at[1, layer], q, other)

    def z_send(layer):
        plane_all(layer).wait_recv()
        total = dw[layer, c, q] + dcore[layer, q]
        for i in range(N_GRP - 1):
            total += xy_r[layer, i].astype(F32)
        zbuf[layer] = total
        for i in range(1, N_Z):
            to = lax.rem(z + i, N_Z)
            rows = pl.ds(pl.multiple_of(to * 16, 16), 16)
            lines[layer, i] = start(remote(
                zbuf.at[layer, rows], z_r.at[layer, i - 1], z_sem.at[0, layer, i - 1], z_sem.at[1, layer, i - 1],
                q, 2 * to + c,
            ))

    mine = pl.ds(pl.multiple_of(z * 16, 16), 16)

    def z_sum(layer):
        total = zbuf[layer, mine, :]
        for i in range(1, N_Z):
            lines[layer, i].wait_recv()
            total += z_r[layer, i - 1]
        slot[layer, mine, :] = (total * scale).astype(BF16)
        for i in range(1, N_Z):
            to = lax.rem(z + i, N_Z)
            spreads[layer, i] = start(remote(
                slot.at[layer, mine], slot.at[layer, mine], ag_sem.at[0, layer, i - 1], ag_sem.at[1, layer, i - 1],
                q, 2 * to + c,
            ))

    def gather(layer):
        for i in range(1, N_Z):
            rows = pl.ds(pl.multiple_of(lax.rem(z + N_Z - i, N_Z) * 16, 16), 16)
            view = slot.at[layer, rows]
            remote(view, view, ag_sem.at[0, layer, i - 1], ag_sem.at[1, layer, i - 1], q, other).wait_recv()
        for i, to in enumerate(ahead):
            wides[layer, i] = start(remote(
                slot.at[layer], gath.at[layer, c, q], agxy_sem.at[0, layer, i], agxy_sem.at[1, layer, i], to, b
            ))
        gath[layer, c, q] = slot[layer]

    def forward(layer):
        for dx in range(4):
            for i, came in enumerate(behind):
                if OFFSETS[i][0] == dx:
                    remote(
                        slot.at[layer], gath.at[layer, c, came], agxy_sem.at[0, layer, i], agxy_sem.at[1, layer, i], q, other
                    ).wait_recv()
            view = gath.at[layer, c, pl.ds(plane(4 - dx, 0) - py, 4)]
            start(remote(view, view, fwd_sem.at[0, layer, dx], fwd_sem.at[1, layer, dx], q, other))

    def finish(layer):
        for dx in range(4):
            view = gath.at[layer, 1 - c, pl.ds(plane(4 - dx, 0) - py, 4)]
            remote(view, view, fwd_sem.at[0, layer, dx], fwd_sem.at[1, layer, dx], q, other).wait_recv()
        for r in range(COEF):
            out_ref[layer, r] = gath[(layer, *slot_of(r))]

    def chains(layer, step):
        for chunk in range(len(CHUNKS)):
            chain(layer, chunk, step)

    front(0)
    loads["w0"].wait()
    edge_back(0)
    outward(0, 0)
    pl.semaphore_wait(barrier, 1 + (N_Z - 1) + (N_GRP - 1))
    core_send(0, 0)
    outward(0, 1)
    core_send(0, 1)
    chain(0, 0, 0)
    outward(0, 2)
    core_send(0, 2)
    chain(0, 1, 0)
    loads["x0"].wait()
    weight_grads(0, ITEMS[:4])
    chain(0, 2, 0)
    weight_grads(0, ITEMS[4:8])
    chains(0, 1)
    weight_grads(0, ITEMS[8:12])
    d_send(0, 0)
    chains(0, 2)
    weight_grads(0, ITEMS[12:])
    d_send(0, 1)
    chains(0, 3)
    chains(0, 4)

    front(1)
    xy_send(0, 0)
    xy_send(0, 1)
    loads["x1"].wait()
    weight_grads(1, PARTS[0])
    d_send(1, 0)
    weight_grads(1, PARTS[1])
    d_send(1, 1)
    loads["w1"].wait()
    edge_back(1)
    xy_send(1, 0)
    outward(1, 0)
    core_send(1, 0)
    xy_send(1, 1)
    outward(1, 1)
    core_send(1, 1)
    z_send(0)
    chain(1, 0, 0)
    outward(1, 2)
    core_send(1, 2)
    chain(1, 1, 0)
    chain(1, 2, 0)
    z_sum(0)
    chains(1, 1)
    z_send(1)
    gather(0)
    chains(1, 2)
    z_sum(1)
    chains(1, 3)
    gather(1)
    chains(1, 4)
    forward(0)
    late = started[-4:] + list(wides.values())
    early = [copy for copy in started if not any(copy is other_copy for other_copy in late)]
    plane_all(0).wait_send()
    plane_all(1).wait_send()
    for copy in early:
        copy.wait_send()
    finish(0)
    forward(1)
    for copy in late + started[-4:]:
        copy.wait_send()
    finish(1)


def both_layers(scale, rot, src, tgt, count, top, x_two, x_one, w_two, w_one):
    dma = pltpu.SemaphoreType.DMA
    vmem = pl.BlockSpec(memory_space=pltpu.VMEM)
    hbm = pl.BlockSpec(memory_space=pltpu.HBM)
    peers = N_GRP - 1
    scratch = [
        pltpu.VMEM((2, COEF, E, C), BF16),
        pltpu.VMEM((2, COEF, C, C), BF16),
        pltpu.VMEM((ROWS, C), F32),
        pltpu.VMEM((AT_ROWS, E), BF16),
        pltpu.VMEM((COEF * C, E), BF16),
        [pltpu.VMEM((width_of(l) * C, height_of(l) * E), BF16) for l in range(7)],
        pltpu.VMEM((N_Z, 2, ROWS, C), F32),
        pltpu.VMEM((2, N_Z, ROWS, C), BF16),
        pltpu.VMEM((2, N_Z, ROWS, C), BF16),
        pltpu.VMEM((2, N_Z - 1, ROWS, C), BF16),
        pltpu.VMEM((2, N_Z - 1, ROWS, C), BF16),
        pltpu.VMEM((2, 2, N_GRP, C, C), F32),
        pltpu.VMEM((2, N_GRP, C, C), F32),
        pltpu.VMEM((2, peers, C, C), BF16),
        pltpu.VMEM((2, peers, C, C), BF16),
        pltpu.VMEM((2, C, C), F32),
        pltpu.VMEM((2, N_Z - 1, 16, C), F32),
        pltpu.VMEM((2, C, C), BF16),
        pltpu.VMEM((2, 2, N_GRP, C, C), BF16),
        dma((4,)),
        dma((2, 2, len(CHUNKS))),
        dma((2, 2, len(CHUNKS), N_Z - 1)),
        dma((2, 2, 2)),
        dma((2, 2)),
        dma((2, 2, N_Z - 1)),
        dma((2, 2, N_Z - 1)),
        dma((2, 2, peers)),
        dma((2, 2, 4)),
    ] + [pltpu.VMEM((2 * C, height_of(l) * E), BF16) for l in range(7)]
    return pl.pallas_call(
        functools.partial(kernel, scale),
        out_shape=(
            jax.ShapeDtypeStruct((LIVE, C), F32),
            pltpu.VMEM((2, COEF, C, C), BF16),
        ),
        in_specs=[vmem] * 5 + [hbm] * 4,
        out_specs=(vmem, vmem),
        scratch_shapes=scratch,
        compiler_params=pltpu.CompilerParams(
            collective_id=0, has_side_effects=True, vmem_limit_bytes=58 * 2**20
        ),
        name="both_layers",
    )(rot, src, tgt, count, top, x_two, x_one, w_two, w_one)


def on_device(
    node_grad, coeffs_one, coeffs_zero, rotations, weight_one, weight_two, sources, targets, edge_count
):
    scale = float(sources.shape[0] * lax.axis_size("grp") * lax.axis_size("bal")) ** (-0.5)
    node, grads = both_layers(
        scale,
        rotations.T,
        sources.reshape(1, E),
        targets.reshape(1, E),
        edge_count.reshape(1, 1),
        jnp.transpose(node_grad, (1, 0, 2)).reshape(LIVE, C),
        jnp.transpose(coeffs_one, (1, 0, 2)),
        jnp.transpose(coeffs_zero, (1, 0, 2)),
        weight_two,
        weight_one,
    )
    node_out = node.reshape(SPHERE, T, C).transpose(1, 0, 2)
    return node_out, grads[1].astype(F32), grads[0].astype(F32)


def solution(mesh):
    both = P(("grp", "bal"))
    return jax.shard_map(
        on_device,
        mesh=mesh,
        in_specs=(
            P(("grp", "bal"), None, None),
            P(("grp", "bal"), None, None),
            P(("grp", "bal"), None, None),
            P(("grp", "bal"), None),
            P(),
            P(),
            both,
            both,
            both,
        ),
        out_specs=(P(("grp", "bal"), None, None), P(), P()),
        check_vma=False,
    )
```

```python
import functools

import jax
import jax.numpy as jnp
from jax import lax
from jax.experimental import pallas as pl
from jax.experimental.pallas import tpu as pltpu
from jax.sharding import PartitionSpec as P

F32, BF16 = jnp.float32, jnp.bfloat16
MESH = pl.DeviceIdType.MESH

C = 128
COEF = 29
SPHERE = 49
WIGNER = 235
E = 256
T = 8
N_GRP = 16
N_Z = 8
ROWS = 400
SLOTS = 32
BASE = (22, 12, 0, 6, 17)
PAIRS = tuple((7 + i, 13 + i) for i in range(6)) + tuple((19 + i, 24 + i) for i in range(5))


def kept_of(degree):
    return min(degree, 2)


def height_of(degree):
    return 2 * kept_of(degree) + 1


def width_of(degree):
    return 2 * degree + 1


def depth_of(degree):
    return 128 if 16 * width_of(degree) <= 128 else 256


STARTS = []
AT_AT = []
_run = 0
_at = 0
for _l in range(7):
    STARTS.append(_run)
    AT_AT.append(_at)
    _run += height_of(_l) * width_of(_l)
    _at += height_of(_l) * depth_of(_l)
AT_ROWS = _at

PLACE = {r: r for r in range(7)}
for _i, (_p, _q) in enumerate(PAIRS):
    PLACE[_p] = 7 + 2 * _i
    PLACE[_q] = 8 + 2 * _i


def dot_nn(a, b):
    return lax.dot_general(a, b, (((1,), (0,)), ((), ())), preferred_element_type=F32)


def dot_nt(a, b):
    return lax.dot_general(a, b, (((1,), (1,)), ((), ())), preferred_element_type=F32)


SINGLES = tuple(range(7))
PARTS = (SINGLES + PAIRS[6:], PAIRS[:6])
ITEMS = PARTS[0] + PARTS[1]
OF_DEGREE = tuple((l,) + ((PAIRS[l - 1],) if l > 0 else ()) + ((PAIRS[l + 4],) if l > 1 else ()) for l in range(7))
PART_SLOTS = ((0, 9), (9, 7))
CHUNKS = (((6,), 288, 112), ((4, 5), 128, 160), ((0, 1, 2, 3), 0, 128))
LIVE = SPHERE * T
OFFSETS = (
    (2, 2), (2, 1), (1, 2), (2, 3), (3, 2), (2, 0), (0, 2), (1, 1),
    (3, 3), (1, 3), (3, 1), (1, 0), (0, 1), (3, 0), (0, 3),
)
HOP = {("a", 4): 0, ("a", 3): 1, ("a", 2): 2, ("a", 1): 3, ("b", 3): 4, ("b", 2): 5, ("b", 1): 6}


def slot_of(r):
    if 7 <= r <= 18 or r >= 30:
        j = r - 7 if r <= 18 else r - 18
        return j // 7, 9 + j % 7
    a = r if r < 7 else r - 12
    return a // 9, a % 9


STEPS = (
    (("a", 4), ("b", 3)), (("a", 3), ("b", 2)), (("a", 2), ("b", 1)), (("a", 1),), (("own", 0),),
)


def remote(src, dst, send, recv, grp, bal):
    return pltpu.make_async_remote_copy(
        src_ref=src, dst_ref=dst, send_sem=send, recv_sem=recv,
        device_id={"grp": grp, "bal": bal}, device_id_type=MESH,
    )


def kernel(
    scale,
    rot_ref, src_ref, tgt_ref, count_ref, top_ref, x_two, x_one, w_two, w_one,
    node_ref, out_ref,
    xs, ws, up, at, gt, sbuf, p, cbuf, crecv, hop_s, hop_r,
    dw, dcore, xy_s, xy_r, zbuf, z_r, slot, gath,
    in_sem, c_sem, hop_sem, d_sem, xy_sem, z_sem, ag_sem, agxy_sem, fwd_sem,
    *dxs,
):
    q = lax.axis_index("grp")
    b = lax.axis_index("bal")
    z, c = lax.div(b, 2), lax.rem(b, 2)
    px, py = lax.div(q, 4), lax.rem(q, 4)
    other = 2 * z + 1 - c

    def plane(dx, dy):
        return lax.rem(px + dx, 4) * 4 + lax.rem(py + dy, 4)

    ahead = [plane(dx, dy) for dx, dy in OFFSETS]
    behind = [plane(4 - dx, 4 - dy) for dx, dy in OFFSETS]

    barrier = pltpu.get_barrier_semaphore()

    def signal(grp, bal):
        pl.semaphore_signal(
            barrier, inc=1, device_id={"grp": grp, "bal": bal}, device_id_type=MESH
        )

    signal(q, other)
    for i in range(1, N_Z):
        signal(q, lax.rem(z + i, N_Z) * 2 + c)
    for to in ahead:
        signal(to, b)

    loads = {}
    for n, (name, src, dst) in enumerate((
        ("w0", w_two, ws.at[0]), ("x0", x_two, xs.at[0]), ("w1", w_one, ws.at[1]), ("x1", x_one, xs.at[1]),
    )):
        loads[name] = pltpu.make_async_copy(src, dst, in_sem.at[n])
        loads[name].start()

    up[0:LIVE] = top_ref[...].astype(F32)
    up[LIVE:ROWS] = jnp.zeros((ROWS - LIVE, C), F32)
    p[:, :, LIVE:ROWS] = jnp.zeros((N_Z, 2, ROWS - LIVE, C), F32)

    def front(layer, degrees):
        if layer == 0:
            lane = lax.broadcasted_iota(jnp.int32, (T, E), 1)
            spot = lax.broadcasted_iota(jnp.int32, (T, E), 0)
            hit = (spot == tgt_ref[...] - b * T) & (lane < count_ref[...])
            hot = jnp.where(hit, 1.0, 0.0).astype(F32)
        for l in degrees:
            width, height, depth = width_of(l), height_of(l), depth_of(l)
            rest = depth - 2 * T * width
            rows = up[T * l * l : T * (l + 1) * (l + 1), :]
            twice = [rows, rows] + ([jnp.zeros((rest, C), F32)] if rest else [])
            ut = jnp.concatenate(twice, 0).T.astype(BF16)
            for m in range(height):
                first = AT_AT[l] + m * depth
                if layer == 0:
                    high, low = [], []
                    for k in range(width):
                        j = STARTS[l] + m * width + k
                        entry = hot * rot_ref[j : j + 1, :]
                        top = entry.astype(BF16).astype(F32)
                        high.append(top)
                        low.append(entry - top)
                    pieces = high + low + ([jnp.zeros((rest, E), F32)] if rest else [])
                    at[first : first + depth, :] = jnp.concatenate(pieces, 0).astype(BF16)
                place = PLACE[BASE[m - kept_of(l) + 2] + l]
                turned = dot_nn(ut, at[first : first + depth, :])
                gt[place * C : (place + 1) * C, :] = turned.astype(BF16)

    def weight_grads(layer, items):
        for item in items:
            if isinstance(item, int):
                g = gt[item * C : (item + 1) * C, :]
                dw[(layer, *slot_of(item))] = dot_nn(g, xs[layer, item])
                continue
            r, s = item
            g = gt[PLACE[r] * C : (PLACE[r] + 2) * C, :]
            both = dot_nn(g, jnp.concatenate([xs[layer, r], xs[layer, s]], 1))
            dw[(layer, *slot_of(r))] = both[:C, :C] + both[C:, C:]
            dw[(layer, *slot_of(s))] = both[C:, :C] - both[:C, C:]

    for layer in range(2):
        for r in range(COEF, SLOTS):
            dw[(layer, *slot_of(r))] = jnp.zeros((C, C), F32)

    def put_dx(r, value):
        high = value.astype(BF16)
        low = (value - high.astype(F32)).astype(BF16)
        for l in range(7):
            for m in range(height_of(l)):
                if BASE[m - kept_of(l) + 2] + l == r:
                    dxs[l][0:C, m * E : (m + 1) * E] = high
                    dxs[l][C : 2 * C, m * E : (m + 1) * E] = low

    def edge_back(layer, degrees):
        for item in [i for l in degrees for i in OF_DEGREE[l]]:
            if isinstance(item, int):
                put_dx(item, dot_nn(ws[layer, item], gt[item * C : (item + 1) * C, :]))
                continue
            r, s = item
            g = gt[PLACE[r] * C : (PLACE[r] + 2) * C, :]
            cosine, sine = ws[layer, r], ws[layer, s]
            block = jnp.concatenate(
                [jnp.concatenate([cosine, sine], 1), jnp.concatenate([-sine, cosine], 1)], 0
            )
            back = dot_nn(block, g)
            put_dx(r, back[:C])
            put_dx(s, back[C:])

    def outward(layer, chunk):
        degrees, begin, count = CHUNKS[chunk]
        for l in degrees:
            width, height = width_of(l), height_of(l)
            if layer == 0:
                nodes = lax.broadcasted_iota(jnp.int32, (C, E), 0)
                at_source = jnp.where(nodes == src_ref[...], 1.0, 0.0).astype(F32)
                for k in range(width):
                    for m in range(height):
                        j = STARTS[l] + m * width + k
                        sbuf[l][k * C : (k + 1) * C, m * E : (m + 1) * E] = (
                            at_source * rot_ref[j : j + 1, :]
                        ).astype(BF16)
            for k0 in range(0, width, 4):
                k1 = min(k0 + 4, width)
                got = dot_nt(sbuf[l][k0 * C : k1 * C, :], dxs[l][...])
                got = got[:, :C] + got[:, C:]
                for k in range(k0, k1):
                    row = l * l + k
                    p[:, :, row * T : (row + 1) * T, :] = got[
                        (k - k0) * C : (k - k0 + 1) * C
                    ].reshape(N_Z, 2, T, C)

    way = jnp.where(c == 0, N_Z - 1, 1)
    step_of = {"a": way, "b": N_Z - way, "own": way}
    started = []

    def start(copy):
        copy.start()
        started.append(copy)
        return copy

    def rows_of(chunk):
        _, begin, count = CHUNKS[chunk]
        return slice(begin, begin + count)

    cores, hops, cross, planes, lines, spreads, wides = {}, {}, {}, {}, {}, {}, {}

    def core_send(layer, chunk):
        rows = rows_of(chunk)
        cbuf[layer, :, rows] = p[:, 1 - c, rows].astype(BF16)
        view = (layer, slice(None), pl.ds(rows.start, rows.stop - rows.start))
        cores[layer, chunk] = start(remote(
            cbuf.at[view], crecv.at[view], c_sem.at[0, layer, chunk], c_sem.at[1, layer, chunk], q, other
        ))

    def chain(layer, chunk, step):
        rows = rows_of(chunk)
        if step == 0:
            cores[layer, chunk].wait_recv()
        for name, dist in STEPS[step]:
            d = lax.rem(z + dist * step_of[name], N_Z)
            value = p[d, c, rows] + crecv[layer, d, rows].astype(F32)
            before = (("a", 1), ("b", 1)) if name == "own" else ((name, dist + 1),)
            for key in before:
                if key in HOP:
                    hops[layer, chunk, key].wait_recv()
                    value += hop_r[layer, HOP[key], rows].astype(F32)
            if name == "own":
                live = min(rows.stop, LIVE) - rows.start
                kept = slice(rows.start, rows.start + live)
                if layer == 0:
                    up[kept] = up[kept] + value[:live]
                else:
                    node_ref[kept] = up[kept] + value[:live]
                continue
            h = HOP[name, dist]
            hop_s[layer, h, rows] = value.astype(BF16)
            view = (layer, h, pl.ds(rows.start, rows.stop - rows.start))
            to = 2 * lax.rem(z + step_of[name], N_Z) + c
            hops[layer, chunk, (name, dist)] = start(remote(
                hop_s.at[view], hop_r.at[view], hop_sem.at[0, layer, chunk, h], hop_sem.at[1, layer, chunk, h], q, to
            ))

    def d_send(layer, part):
        first, count = PART_SLOTS[part]
        view = pl.ds(first, count)
        cross[layer, part] = start(remote(
            dw.at[layer, 1 - c, view], dcore.at[layer, view], d_sem.at[0, layer, part], d_sem.at[1, layer, part], q, other
        ))

    def xy_send(layer, part):
        cross[layer, part].wait_recv()
        first, count = PART_SLOTS[part]
        for i in range(count):
            to = first + lax.rem(q + i, count)

            @pl.when(to != q)
            def _():
                there = lax.rem(to - q + N_GRP, N_GRP) - 1
                here = lax.rem(q - to + N_GRP, N_GRP) - 1
                xy_s[layer, there] = (dw[layer, c, to] + dcore[layer, to]).astype(BF16)
                remote(
                    xy_s.at[layer, there], xy_r.at[layer, here], xy_sem.at[0, layer], xy_sem.at[1, layer], to, b
                ).start()

    def plane_all(layer):
        return remote(xy_s.at[layer], xy_r.at[layer], xy_sem.at[0, layer], xy_sem.at[1, layer], q, other)

    def z_send(layer):
        plane_all(layer).wait_recv()
        total = dw[layer, c, q] + dcore[layer, q]
        for i in range(N_GRP - 1):
            total += xy_r[layer, i].astype(F32)
        zbuf[layer] = total.T
        for i in range(1, N_Z):
            to = lax.rem(z + i, N_Z)
            rows = pl.ds(pl.multiple_of(to * 16, 16), 16)
            lines[layer, i] = start(remote(
                zbuf.at[layer, rows], z_r.at[layer, i - 1], z_sem.at[0, layer, i - 1], z_sem.at[1, layer, i - 1],
                q, 2 * to + c,
            ))

    mine = pl.ds(pl.multiple_of(z * 16, 16), 16)

    def z_sum(layer):
        total = zbuf[layer, mine, :]
        for i in range(1, N_Z):
            lines[layer, i].wait_recv()
            total += z_r[layer, i - 1]
        slot[layer, mine, :] = (total * scale).astype(BF16)
        for i in range(1, N_Z):
            to = lax.rem(z + i, N_Z)
            spreads[layer, i] = start(remote(
                slot.at[layer, mine], slot.at[layer, mine], ag_sem.at[0, layer, i - 1], ag_sem.at[1, layer, i - 1],
                q, 2 * to + c,
            ))

    def gather(layer):
        for i in range(1, N_Z):
            rows = pl.ds(pl.multiple_of(lax.rem(z + N_Z - i, N_Z) * 16, 16), 16)
            view = slot.at[layer, rows]
            remote(view, view, ag_sem.at[0, layer, i - 1], ag_sem.at[1, layer, i - 1], q, other).wait_recv()
        for i, to in enumerate(ahead):
            wides[layer, i] = start(remote(
                slot.at[layer], gath.at[layer, c, q], agxy_sem.at[0, layer, i], agxy_sem.at[1, layer, i], to, b
            ))
        gath[layer, c, q] = slot[layer]

    def forward(layer):
        for dx in range(4):
            for i, came in enumerate(behind):
                if OFFSETS[i][0] == dx:
                    remote(
                        slot.at[layer], gath.at[layer, c, came], agxy_sem.at[0, layer, i], agxy_sem.at[1, layer, i], q, other
                    ).wait_recv()
            view = gath.at[layer, c, pl.ds(plane(4 - dx, 0) - py, 4)]
            start(remote(view, view, fwd_sem.at[0, layer, dx], fwd_sem.at[1, layer, dx], q, other))

    def finish(layer):
        for dx in range(4):
            view = gath.at[layer, 1 - c, pl.ds(plane(4 - dx, 0) - py, 4)]
            remote(view, view, fwd_sem.at[0, layer, dx], fwd_sem.at[1, layer, dx], q, other).wait_recv()
        for r in range(COEF):
            out_ref[layer, r] = gath[(layer, *slot_of(r))]

    def chains(layer, step):
        for chunk in range(len(CHUNKS)):
            chain(layer, chunk, step)

    def back_chunk(layer, chunk):
        edge_back(layer, CHUNKS[chunk][0])
        outward(layer, chunk)

    front(0, CHUNKS[0][0])
    loads["w0"].wait()
    back_chunk(0, 0)
    pl.semaphore_wait(barrier, 1 + (N_Z - 1) + (N_GRP - 1))
    core_send(0, 0)
    front(0, CHUNKS[1][0])
    back_chunk(0, 1)
    core_send(0, 1)
    chain(0, 0, 0)
    front(0, CHUNKS[2][0])
    back_chunk(0, 2)
    core_send(0, 2)
    chain(0, 1, 0)
    loads["x0"].wait()
    weight_grads(0, PARTS[0])
    d_send(0, 0)
    chain(0, 2, 0)
    chains(0, 1)
    weight_grads(0, PARTS[1])
    d_send(0, 1)
    chains(0, 2)
    xy_send(0, 0)
    xy_send(0, 1)
    chains(0, 3)
    chain(0, 0, 4)
    front(1, CHUNKS[0][0])
    chain(0, 1, 4)

    front(1, CHUNKS[1][0])
    chain(0, 2, 4)
    front(1, CHUNKS[2][0])
    loads["x1"].wait()
    weight_grads(1, PARTS[0])
    d_send(1, 0)
    weight_grads(1, PARTS[1])
    d_send(1, 1)
    z_send(0)
    loads["w1"].wait()
    back_chunk(1, 0)
    core_send(1, 0)
    xy_send(1, 0)
    back_chunk(1, 1)
    core_send(1, 1)
    xy_send(1, 1)
    chain(1, 0, 0)
    back_chunk(1, 2)
    core_send(1, 2)
    chain(1, 1, 0)
    chain(1, 2, 0)
    z_sum(0)
    chains(1, 1)
    z_send(1)
    gather(0)
    chains(1, 2)
    z_sum(1)
    chains(1, 3)
    gather(1)
    chains(1, 4)
    forward(0)
    late = started[-4:] + list(wides.values())
    early = [copy for copy in started if not any(copy is other_copy for other_copy in late)]
    plane_all(0).wait_send()
    plane_all(1).wait_send()
    for copy in early:
        copy.wait_send()
    finish(0)
    forward(1)
    for copy in late + started[-4:]:
        copy.wait_send()
    finish(1)


def both_layers(scale, rot, src, tgt, count, top, x_two, x_one, w_two, w_one):
    dma = pltpu.SemaphoreType.DMA
    vmem = pl.BlockSpec(memory_space=pltpu.VMEM)
    hbm = pl.BlockSpec(memory_space=pltpu.HBM)
    peers = N_GRP - 1
    scratch = [
        pltpu.VMEM((2, COEF, E, C), BF16),
        pltpu.VMEM((2, COEF, C, C), BF16),
        pltpu.VMEM((ROWS, C), F32),
        pltpu.VMEM((AT_ROWS, E), BF16),
        pltpu.VMEM((COEF * C, E), BF16),
        [pltpu.VMEM((width_of(l) * C, height_of(l) * E), BF16) for l in range(7)],
        pltpu.VMEM((N_Z, 2, ROWS, C), F32),
        pltpu.VMEM((2, N_Z, ROWS, C), BF16),
        pltpu.VMEM((2, N_Z, ROWS, C), BF16),
        pltpu.VMEM((2, N_Z - 1, ROWS, C), BF16),
        pltpu.VMEM((2, N_Z - 1, ROWS, C), BF16),
        pltpu.VMEM((2, 2, N_GRP, C, C), F32),
        pltpu.VMEM((2, N_GRP, C, C), F32),
        pltpu.VMEM((2, peers, C, C), BF16),
        pltpu.VMEM((2, peers, C, C), BF16),
        pltpu.VMEM((2, C, C), F32),
        pltpu.VMEM((2, N_Z - 1, 16, C), F32),
        pltpu.VMEM((2, C, C), BF16),
        pltpu.VMEM((2, 2, N_GRP, C, C), BF16),
        dma((4,)),
        dma((2, 2, len(CHUNKS))),
        dma((2, 2, len(CHUNKS), N_Z - 1)),
        dma((2, 2, 2)),
        dma((2, 2)),
        dma((2, 2, N_Z - 1)),
        dma((2, 2, N_Z - 1)),
        dma((2, 2, peers)),
        dma((2, 2, 4)),
    ] + [pltpu.VMEM((2 * C, height_of(l) * E), BF16) for l in range(7)]
    return pl.pallas_call(
        functools.partial(kernel, scale),
        out_shape=(
            jax.ShapeDtypeStruct((LIVE, C), F32),
            pltpu.VMEM((2, COEF, C, C), BF16),
        ),
        in_specs=[vmem] * 5 + [hbm] * 4,
        out_specs=(vmem, vmem),
        scratch_shapes=scratch,
        compiler_params=pltpu.CompilerParams(
            collective_id=0, has_side_effects=True, vmem_limit_bytes=58 * 2**20
        ),
        name="both_layers",
    )(rot, src, tgt, count, top, x_two, x_one, w_two, w_one)


def on_device(
    node_grad, coeffs_one, coeffs_zero, rotations, weight_one, weight_two, sources, targets, edge_count
):
    scale = float(sources.shape[0] * lax.axis_size("grp") * lax.axis_size("bal")) ** (-0.5)
    node, grads = both_layers(
        scale,
        rotations.T,
        sources.reshape(1, E),
        targets.reshape(1, E),
        edge_count.reshape(1, 1),
        jnp.transpose(node_grad, (1, 0, 2)).reshape(LIVE, C),
        jnp.transpose(coeffs_one, (1, 0, 2)),
        jnp.transpose(coeffs_zero, (1, 0, 2)),
        weight_two,
        weight_one,
    )
    node_out = node.reshape(SPHERE, T, C).transpose(1, 0, 2)
    return node_out, grads[1].astype(F32), grads[0].astype(F32)


def solution(mesh):
    both = P(("grp", "bal"))
    return jax.shard_map(
        on_device,
        mesh=mesh,
        in_specs=(
            P(("grp", "bal"), None, None),
            P(("grp", "bal"), None, None),
            P(("grp", "bal"), None, None),
            P(("grp", "bal"), None),
            P(),
            P(),
            both,
            both,
            both,
        ),
        out_specs=(P(("grp", "bal"), None, None), P(), P()),
        check_vma=False,
    )
```
